128 devices in a mesh: row: 8 (over x, core), col: 16 (over y, z).
Axes of the slice: x: 4, y: 4, z: 4, core: 2. Of those that a mesh axis runs over, the one named last changes fastest.
Arguments:
- front: bfloat16 [24576, 24576], P('row', 'col'), may hold values from -6 to 6
- diag_inverse: bfloat16 [256, 256], replicated, as said below
- fill_pattern: int32 [384, 384], replicated, may hold values from 0 to 1, as said below
Outputs:
- updated: bfloat16 [24576, 24576], P('row', 'col')
The draws below stay inside these ranges and needn't reach their ends.
Inputs may be any that keep to these rules, and one draw needn't show every extreme that they name: `fill_pattern`: symmetric, with ones on the diagonal. `diag_inverse`: lower triangular.
All inputs are finite; a program needn't handle non-finite values.
Results may differ from the reference program's by a relative error of at most 0.0045.
Values may be sent and summed in bfloat16 or wider, within the bound.
No kernel may reach another device: no remote copies, remote signals or barrier semaphores. Data moves between devices by JAX's collectives and lax.ppermute only.
A program may use at most 128 MiB of HBM per device.

```python
import jax
import jax.numpy as jnp
from jax import lax

M = 24576
B = 64
P_SIZE = 256
N_ROW = 8
N_COL = 16


def draw_fill_pattern(key, part):
    count = M // B
    values = jax.random.randint(key, (count, count), 0, 4)
    marks = (values < 3).astype(jnp.int32)
    both = marks * marks.T
    ident = jnp.eye(count, dtype=jnp.int32)
    return jnp.maximum(both, ident)


def draw_diag_inverse(key, part):
    first = jax.random.fold_in(key, 0)
    values = jax.random.normal(first, (P_SIZE, P_SIZE), jnp.float32)
    scales = jnp.ones((P_SIZE, 1), jnp.float32)
    index = jnp.arange(P_SIZE, dtype=jnp.int32)
    lower = (index[:, None] >= index[None, :]).astype(jnp.float32)
    counts = (index + 1).astype(jnp.float32)[:, None]
    weights = 0.25 * scales * values * lower / jnp.sqrt(counts)
    weights = weights + 0.2 * jnp.eye(P_SIZE, dtype=jnp.float32)
    return weights.astype(jnp.bfloat16)


def block_levels(stream_key, shape, shards, least, high):
    def one(position, parts):
        heights = jax.random.uniform(jax.random.fold_in(jax.random.fold_in(stream_key, 6), position), (parts,), jnp.float32, least / len(shards), high / len(shards))
        return jnp.repeat(jnp.exp(heights), shape[position] // parts).reshape((-1,) + (1,) * (len(shape) - position - 1))

    loudness = one(*shards[0])
    for cut in shards[1:]:
        loudness = loudness * one(*cut)
    return loudness


def bell_draw(key, shape, scale, limit, cuts=(), held_as=jnp.bfloat16):
    loudness = block_levels(key, shape, cuts, -0.22, 0.18) if cuts else 1.0
    result = jax.random.normal(key, shape, jnp.float32) * scale * loudness
    return jnp.minimum(jnp.maximum(result, -limit), limit).astype(held_as)


def setup_inputs(seed: int = 0) -> dict:
    streams_of = jax.random.split(jax.random.key(seed), 4)
    front = bell_draw(streams_of[0], (M, M), 1.0, 6.0, ((0, 8), (1, 16)))
    diag_inverse = draw_diag_inverse(jax.random.fold_in(streams_of[3], 71), 0)
    fill_pattern = draw_fill_pattern(jax.random.fold_in(streams_of[3], 71), 0)
    return dict(front=front, diag_inverse=diag_inverse, fill_pattern=fill_pattern)


def reference(front, diag_inverse, fill_pattern):
    blocks = M // B
    local_rows = M // (B * N_ROW)
    local_cols = M // (B * N_COL)
    panel_blocks = P_SIZE // B
    stored = jnp.arange(blocks, dtype=jnp.int32)
    row_global = (stored % local_rows) * N_ROW + stored // local_rows
    col_global = (stored % local_cols) * N_COL + stored // local_cols
    panel = jnp.concatenate([front[:, h * local_cols * B:h * local_cols * B + B] for h in range(panel_blocks)], axis=1)
    factor = jnp.dot(panel, diag_inverse.T, preferred_element_type=jnp.float32).astype(jnp.bfloat16)
    source = (col_global % N_ROW) * local_rows + col_global // N_ROW
    col_factor = factor.reshape(blocks, B, P_SIZE)[source].reshape(M, P_SIZE)
    keep = fill_pattern[row_global][:, col_global].astype(jnp.float32)
    keep = keep * (row_global >= panel_blocks).astype(jnp.float32)[:, None]
    keep = keep * (col_global >= panel_blocks).astype(jnp.float32)[None, :]

    def one_block(items):
        front_rows, factor_rows, keep_row = items
        product = jnp.dot(factor_rows, col_factor.T, preferred_element_type=jnp.float32)
        spread = jnp.repeat(keep_row, B)
        return (front_rows.astype(jnp.float32) - product * spread[None, :]).astype(jnp.bfloat16)

    updated = lax.map(one_block, (front.reshape(blocks, B, M), factor.reshape(blocks, B, P_SIZE), keep))
    updated = updated.reshape(M, M)
    for h in range(panel_blocks):
        updated = updated.at[:, h * local_cols * B:h * local_cols * B + B].set(factor[:, h * B:(h + 1) * B])
    return updated
```

```python
import functools

import jax
import jax.numpy as jnp
import numpy as np
from jax import lax
from jax.experimental import pallas as pl
from jax.experimental.pallas import tpu as pltpu
from jax.sharding import Mesh, PartitionSpec as P

BF16 = jnp.bfloat16
F32 = jnp.float32
B = 64
Q = 4
BLOCKS = 48
PAIRS = 24
HALF = 12
ROWS = HALF * B
COLS = 1536
WIDTH = 256
ALL = ("x", "core", "y", "z")
VMEM = pltpu.VMEM
NT = (((1,), (1,)), ((), ()))


def linear(x, core, y, z):
    return ((x * 2 + core) * 4 + y) * 4 + z


def quarter_of(y, z):
    return (z + 2 * (y // 2)) % 4


def spread_perm(step):
    pairs = []
    for x in range(4):
        for core in range(2):
            for j in range(4):
                target = [(1, j), (2, (j + 2) % 4), (3, (j + 2) % 4)][step]
                pairs.append((linear(x, core, 0, j), linear(x, core, *target)))
    return pairs


def column_perm(step):
    pairs = []
    for x in range(4):
        for core in range(2):
            r = 2 * x + core
            for y in range(4):
                for z in range(4):
                    q = quarter_of(y, z)
                    half = step if q < 2 else 1 - step
                    target = linear((y + x) % 4, q % 2, 2 * half + r // 4, r % 4)
                    pairs.append((linear(x, core, y, z), target))
    return pairs


def pack_kernel(front_ref, out_ref):
    flip = lax.axis_index("z") // 2
    for k in range(2):
        parity = jnp.bitwise_xor(k, flip)
        left = front_ref[:HALF, parity, :, :].reshape(ROWS, 128)
        right = front_ref[HALF:, parity, :, :].reshape(ROWS, 128)
        out_ref[k] = jnp.concatenate([left[:, :B], right[:, :B]], axis=1)


def pack(front4):
    return pl.pallas_call(
        pack_kernel,
        grid=(1,),
        out_shape=jax.ShapeDtypeStruct((2, ROWS, 128), BF16),
        in_specs=[pl.BlockSpec((PAIRS, 2, B, 128), lambda i: (0, 0, 0, 0))],
        out_specs=pl.BlockSpec((2, ROWS, 128), lambda i: (0, 0, 0)),
        compiler_params=pltpu.CompilerParams(vmem_limit_bytes=16 << 20),
    )(front4)


def choose_kernel(a_ref, b_ref, c_ref, d_ref, own_ref, first_ref, second_ref):
    y = lax.axis_index("y")
    for k, ref in enumerate((a_ref, b_ref, c_ref, d_ref)):

        @pl.when(y == k)
        def _():
            own_ref[...] = ref[...]
            first_ref[...] = ref[0]
            second_ref[...] = ref[1]


def choose(a, b, c, d):
    whole = pl.BlockSpec(memory_space=VMEM)
    return pl.pallas_call(
        choose_kernel,
        out_shape=(
            jax.ShapeDtypeStruct((2, ROWS, 128), BF16),
            jax.ShapeDtypeStruct((ROWS, 128), BF16),
            jax.ShapeDtypeStruct((ROWS, 128), BF16),
        ),
        in_specs=[whole] * 4,
        out_specs=(whole,) * 3,
        compiler_params=pltpu.CompilerParams(vmem_limit_bytes=16 << 20),
    )(a, b, c, d)


def prepare_kernel(diag_ref, pattern_ref, row_w_ref, col_w_ref, mask_ref):
    x, core = lax.axis_index("x"), lax.axis_index("core")
    y, z = lax.axis_index("y"), lax.axis_index("z")
    own = lax.rem(z + 2 * (y // 2), 4)
    diag = diag_ref[...]
    eye = (
        lax.broadcasted_iota(jnp.int32, (WIDTH, WIDTH), 0)
        == lax.broadcasted_iota(jnp.int32, (WIDTH, WIDTH), 1)
    ).astype(BF16)
    turned = lax.dot_general(eye, diag, NT, preferred_element_type=F32).astype(BF16)
    for q in range(Q):
        slot = lax.rem(q - own + 4, 4)
        part = turned[q * B : q * B + B, :]
        zero = jnp.zeros_like(part)
        row_w_ref[0, slot] = jnp.concatenate([part, zero], axis=0)
        row_w_ref[1, slot] = jnp.concatenate([zero, part], axis=0)
        half = y // 2
        other = jnp.where(q % 2 == core, 0, 2)
        late = jnp.where(q // 2 == half, 0, 1)
        part = diag[:, q * B : q * B + B]
        zero = jnp.zeros_like(part)
        col_w_ref[0, other + late] = jnp.concatenate([part, zero], axis=1)
        col_w_ref[1, other + late] = jnp.concatenate([zero, part], axis=1)
    row_id = x * 2 + core
    col_id = y * 4 + z
    count = pattern_ref.shape[0]
    rows = (
        lax.broadcasted_iota(jnp.int32, (BLOCKS, count), 0) * 8 + row_id
        == lax.broadcasted_iota(jnp.int32, (BLOCKS, count), 1)
    ).astype(BF16)
    cols = (
        lax.broadcasted_iota(jnp.int32, (count, COLS), 0)
        == lax.broadcasted_iota(jnp.int32, (count, COLS), 1) // B * 16 + col_id
    ).astype(BF16)
    picked = jnp.dot(
        rows, pattern_ref[...].astype(F32).astype(BF16), preferred_element_type=F32
    ).astype(BF16)
    keep = jnp.dot(picked, cols, preferred_element_type=F32)
    stored_row = lax.broadcasted_iota(jnp.int32, (BLOCKS, COLS), 0)
    stored_col = lax.broadcasted_iota(jnp.int32, (BLOCKS, COLS), 1) // B
    inside = (stored_row * 8 + row_id >= Q) & (stored_col * 16 + col_id >= Q)
    mask_ref[...] = jnp.where(inside, keep, 0.0)


def prepare(diag_inverse, fill_pattern):
    whole = pl.BlockSpec(memory_space=VMEM)
    return pl.pallas_call(
        prepare_kernel,
        out_shape=(
            jax.ShapeDtypeStruct((2, Q, 128, WIDTH), BF16),
            jax.ShapeDtypeStruct((2, Q, WIDTH, 128), BF16),
            jax.ShapeDtypeStruct((BLOCKS, COLS), F32),
        ),
        in_specs=[whole] * 2,
        out_specs=(whole,) * 3,
        compiler_params=pltpu.CompilerParams(vmem_limit_bytes=24 << 20),
    )(diag_inverse, fill_pattern)


TILE = 4
CHUNK = 512


def update_kernel(
    front_ref, p0, p1, p2, p3, g0, g1, g2, g3, row_w_ref, col_w_ref, mask_ref, out_ref, gt_ref
):
    parity, i = pl.program_id(0), pl.program_id(1)
    y, z = lax.axis_index("y"), lax.axis_index("z")
    col_id = y * 4 + z
    owner = col_id < Q
    own = lax.rem(z + 2 * (y // 2), 4)

    @pl.when((parity == 0) & (i == 0))
    def _():
        for u in range(2):
            total = jnp.zeros((WIDTH, ROWS), F32)
            for k, g in enumerate((g0, g1, g2, g3)):
                total += lax.dot_general(
                    col_w_ref[u, k], g[...], NT, preferred_element_type=F32
                )
            gt_ref[:, u * ROWS : (u + 1) * ROWS] = total.astype(BF16)

        @pl.when(owner)
        def _():
            lane = lax.broadcasted_iota(jnp.int32, (WIDTH, 128), 1)
            line = lax.broadcasted_iota(jnp.int32, (WIDTH, 128), 0)
            pick = (line == lane + col_id * B).astype(F32)
            old = gt_ref[:, :128].astype(F32)
            gt_ref[:, :128] = jnp.where(lane < B, pick, old).astype(BF16)

    u = i // (HALF // TILE)
    start = pl.multiple_of(lax.rem(i, HALF // TILE) * (TILE * B), TILE * B)
    total = jnp.zeros((TILE * B, WIDTH), F32)
    for k, p in enumerate((p0, p1, p2, p3)):
        q = lax.rem(own + k, 4)
        slot = jnp.bitwise_xor(parity, q // 2)
        total += jnp.dot(
            p[slot, pl.ds(start, TILE * B), :], row_w_ref[u, k], preferred_element_type=F32
        )
    factor = total.astype(BF16)
    lane = lax.broadcasted_iota(jnp.int32, (B, CHUNK), 1)
    for c in range(COLS // CHUNK):
        cols = slice(c * CHUNK, (c + 1) * CHUNK)
        product = jnp.dot(factor, gt_ref[:, cols], preferred_element_type=F32)
        for b in range(TILE):
            part = product[b * B : b * B + B]
            keep = mask_ref[pl.ds(2 * (TILE * i + b) + parity, 1), cols]
            new = front_ref[b, 0, :, cols].astype(F32) - part * keep
            if c == 0:
                new = jnp.where(owner & (lane < B), part, new)
            out_ref[b, 0, :, cols] = new.astype(BF16)


def update(front4, parts, columns, row_w, col_w, mask):
    whole = pl.BlockSpec(memory_space=VMEM)
    tile = pl.BlockSpec((TILE, 1, B, COLS), lambda p, i: (i, p, 0, 0))
    return pl.pallas_call(
        update_kernel,
        grid=(2, PAIRS // TILE),
        out_shape=jax.ShapeDtypeStruct((PAIRS, 2, B, COLS), BF16),
        in_specs=[tile] + [whole] * 11,
        out_specs=tile,
        scratch_shapes=[VMEM((WIDTH, COLS), BF16)],
        compiler_params=pltpu.CompilerParams(vmem_limit_bytes=32 << 20),
        cost_estimate=pl.CostEstimate(
            flops=2 * 3072 * 1536 * 256, bytes_accessed=4 * 3072 * 1536, transcendentals=0
        ),
    )(front4, *parts, *columns, row_w, col_w, mask)


def body(front, diag_inverse, fill_pattern):
    front4 = front.reshape(PAIRS, 2, B, COLS)
    packed = pack(front4)
    row_w, col_w, mask = prepare(diag_inverse, fill_pattern)
    spread = [lax.ppermute(packed, ALL, spread_perm(k)) for k in range(3)]
    own, first, second = choose(packed, *spread)
    g0 = lax.ppermute(first, ALL, column_perm(0))
    g1 = lax.ppermute(second, ALL, column_perm(1))
    z_next = lax.ppermute(own, "z", [((i + 1) % 4, i) for i in range(4)])
    z_prev = lax.ppermute(own, "z", [(i, (i + 1) % 4) for i in range(4)])
    y_pair = lax.ppermute(own, "y", [(1, 2), (2, 1), (3, 0), (0, 3)])
    swap = [(0, 1), (1, 0)]
    g2 = lax.ppermute(g0, "core", swap)
    g3 = lax.ppermute(g1, "core", swap)
    out = update(
        front4, (own, z_next, y_pair, z_prev), (g0, g1, g2, g3), row_w, col_w, mask
    )
    return out.reshape(front.shape)


def solution(mesh):
    fine = Mesh(mesh.devices.reshape(4, 2, 4, 4), ALL)
    spec = P(("x", "core"), ("y", "z"))
    return jax.shard_map(
        body,
        mesh=fine,
        in_specs=(spec, P(), P()),
        out_specs=spec,
        check_vma=False,
    )
```

```python
import functools

import jax
import jax.numpy as jnp
import numpy as np
from jax import lax
from jax.experimental import pallas as pl
from jax.experimental.pallas import tpu as pltpu
from jax.sharding import Mesh, PartitionSpec as P

BF16 = jnp.bfloat16
F32 = jnp.float32
B = 64
Q = 4
BLOCKS = 48
PAIRS = 24
HALF = 12
ROWS = HALF * B
COLS = 1536
WIDTH = 256
ALL = ("x", "core", "y", "z")
VMEM = pltpu.VMEM
NT = (((1,), (1,)), ((), ()))


def linear(x, core, y, z):
    return ((x * 2 + core) * 4 + y) * 4 + z


def quarter_of(y, z):
    return (z + 2 * (y // 2)) % 4


def spread_perm(step):
    pairs = []
    for x in range(4):
        for core in range(2):
            for j in range(4):
                target = [(1, j), (2, (j + 2) % 4), (3, (j + 2) % 4)][step]
                pairs.append((linear(x, core, 0, j), linear(x, core, *target)))
    return pairs


def column_perm(step):
    pairs = []
    for x in range(4):
        for core in range(2):
            r = 2 * x + core
            for y in range(4):
                for z in range(4):
                    q = quarter_of(y, z)
                    half = step if q < 2 else 1 - step
                    target = linear((y + x) % 4, q % 2, 2 * half + r // 4, r % 4)
                    pairs.append((linear(x, core, y, z), target))
    return pairs


def pack_kernel(panel_ref, out_ref):
    flip = lax.axis_index("z") // 2
    for k in range(2):
        parity = jnp.bitwise_xor(k, flip)
        left = panel_ref[:HALF, parity, :, :].reshape(ROWS, 128)
        right = panel_ref[HALF:, parity, :, :].reshape(ROWS, 128)
        out_ref[k] = jnp.concatenate([left[:, :B], right[:, :B]], axis=1)


def pack(panel4):
    whole = pl.BlockSpec(memory_space=VMEM)
    return pl.pallas_call(
        pack_kernel,
        out_shape=jax.ShapeDtypeStruct((2, ROWS, 128), BF16),
        in_specs=[whole],
        out_specs=whole,
        compiler_params=pltpu.CompilerParams(vmem_limit_bytes=16 << 20),
    )(panel4)


def choose_kernel(a_ref, b_ref, c_ref, d_ref, own_ref, first_ref, second_ref):
    y = lax.axis_index("y")
    for k, ref in enumerate((a_ref, b_ref, c_ref, d_ref)):

        @pl.when(y == k)
        def _():
            own_ref[...] = ref[...]
            first_ref[...] = ref[0]
            second_ref[...] = ref[1]


def choose(a, b, c, d):
    whole = pl.BlockSpec(memory_space=VMEM)
    return pl.pallas_call(
        choose_kernel,
        out_shape=(
            jax.ShapeDtypeStruct((2, ROWS, 128), BF16),
            jax.ShapeDtypeStruct((ROWS, 128), BF16),
            jax.ShapeDtypeStruct((ROWS, 128), BF16),
        ),
        in_specs=[whole] * 4,
        out_specs=(whole,) * 3,
        compiler_params=pltpu.CompilerParams(vmem_limit_bytes=16 << 20),
    )(a, b, c, d)


STAGES = 4


def prepare_kernel(
    front_ref, diag_ref, pattern_ref, row_w_ref, col_w_ref, mask_ref, stay_ref, sems
):
    span = PAIRS // STAGES
    copies = []
    for k in range(STAGES):
        part = pl.ds(k * span, span)
        copies.append(
            pltpu.make_async_copy(front_ref.at[part], stay_ref.at[part], sems.at[k])
        )
        copies[-1].start()
    x, core = lax.axis_index("x"), lax.axis_index("core")
    y, z = lax.axis_index("y"), lax.axis_index("z")
    own = lax.rem(z + 2 * (y // 2), 4)
    diag = diag_ref[...]
    eye = (
        lax.broadcasted_iota(jnp.int32, (WIDTH, WIDTH), 0)
        == lax.broadcasted_iota(jnp.int32, (WIDTH, WIDTH), 1)
    ).astype(BF16)
    turned = lax.dot_general(eye, diag, NT, preferred_element_type=F32).astype(BF16)
    for q in range(Q):
        slot = lax.rem(q - own + 4, 4)
        part = turned[q * B : q * B + B, :]
        zero = jnp.zeros_like(part)
        row_w_ref[0, slot] = jnp.concatenate([part, zero], axis=0)
        row_w_ref[1, slot] = jnp.concatenate([zero, part], axis=0)
        half = y // 2
        other = jnp.where(q % 2 == core, 0, 2)
        late = jnp.where(q // 2 == half, 0, 1)
        part = diag[:, q * B : q * B + B]
        zero = jnp.zeros_like(part)
        col_w_ref[0, other + late] = jnp.concatenate([part, zero], axis=1)
        col_w_ref[1, other + late] = jnp.concatenate([zero, part], axis=1)
    row_id = x * 2 + core
    col_id = y * 4 + z
    count = pattern_ref.shape[0]
    rows = (
        lax.broadcasted_iota(jnp.int32, (BLOCKS, count), 0) * 8 + row_id
        == lax.broadcasted_iota(jnp.int32, (BLOCKS, count), 1)
    ).astype(BF16)
    cols = (
        lax.broadcasted_iota(jnp.int32, (count, COLS), 0)
        == lax.broadcasted_iota(jnp.int32, (count, COLS), 1) // B * 16 + col_id
    ).astype(BF16)
    picked = jnp.dot(
        rows, pattern_ref[...].astype(F32).astype(BF16), preferred_element_type=F32
    ).astype(BF16)
    keep = jnp.dot(picked, cols, preferred_element_type=F32)
    stored_row = lax.broadcasted_iota(jnp.int32, (BLOCKS, COLS), 0)
    stored_col = lax.broadcasted_iota(jnp.int32, (BLOCKS, COLS), 1) // B
    inside = (stored_row * 8 + row_id >= Q) & (stored_col * 16 + col_id >= Q)
    mask_ref[...] = jnp.where(inside, keep, 0.0)
    for copy in copies:
        copy.wait()


def prepare(front4, diag_inverse, fill_pattern):
    whole = pl.BlockSpec(memory_space=VMEM)
    return pl.pallas_call(
        prepare_kernel,
        out_shape=(
            jax.ShapeDtypeStruct((2, Q, 128, WIDTH), BF16),
            jax.ShapeDtypeStruct((2, Q, WIDTH, 128), BF16),
            jax.ShapeDtypeStruct((BLOCKS, COLS), F32),
            jax.ShapeDtypeStruct(front4.shape, BF16),
        ),
        in_specs=[pl.BlockSpec(memory_space=pltpu.HBM), whole, whole],
        out_specs=(whole,) * 4,
        scratch_shapes=[pltpu.SemaphoreType.DMA((STAGES,))],
        compiler_params=pltpu.CompilerParams(vmem_limit_bytes=41 << 20),
        cost_estimate=pl.CostEstimate(
            flops=0, bytes_accessed=2 * 3072 * 1536 * 2, transcendentals=0
        ),
    )(front4, diag_inverse, fill_pattern)


def column_kernel(g0, g1, g2, g3, col_w_ref, out_ref):
    col_id = lax.axis_index("y") * 4 + lax.axis_index("z")
    for u in range(2):
        total = jnp.zeros((WIDTH, ROWS), F32)
        for k, g in enumerate((g0, g1, g2, g3)):
            total += lax.dot_general(col_w_ref[u, k], g[...], NT, preferred_element_type=F32)
        out_ref[:, u * ROWS : (u + 1) * ROWS] = total.astype(BF16)

    @pl.when(col_id < Q)
    def _():
        lane = lax.broadcasted_iota(jnp.int32, (WIDTH, 128), 1)
        line = lax.broadcasted_iota(jnp.int32, (WIDTH, 128), 0)
        pick = (line == lane + col_id * B).astype(F32)
        old = out_ref[:, :128].astype(F32)
        out_ref[:, :128] = jnp.where(lane < B, pick, old).astype(BF16)


def column_factor(columns, col_w):
    whole = pl.BlockSpec(memory_space=VMEM)
    return pl.pallas_call(
        column_kernel,
        out_shape=jax.ShapeDtypeStruct((WIDTH, COLS), BF16),
        in_specs=[whole] * 5,
        out_specs=whole,
        compiler_params=pltpu.CompilerParams(vmem_limit_bytes=16 << 20),
        cost_estimate=pl.CostEstimate(
            flops=2 * COLS * 256 * 512, bytes_accessed=2 * COLS * 768, transcendentals=0
        ),
    )(*columns, col_w)


CHUNK = 512


def update_kernel(front_ref, p0, p1, p2, p3, gt_ref, row_w_ref, mask_ref, out_ref):
    parity, u = pl.program_id(0), pl.program_id(1)
    y, z = lax.axis_index("y"), lax.axis_index("z")
    owner = y * 4 + z < Q
    own = lax.rem(z + 2 * (y // 2), 4)
    parts = []
    for k, p in enumerate((p0, p1, p2, p3)):
        q = lax.rem(own + k, 4)
        parts.append(p[jnp.bitwise_xor(parity, q // 2)])
    factor = jnp.dot(
        jnp.concatenate(parts, axis=1),
        row_w_ref[u].reshape(Q * 128, WIDTH),
        preferred_element_type=F32,
    ).astype(BF16)
    lane = lax.broadcasted_iota(jnp.int32, (B, 128), 1)
    for c in range(COLS // CHUNK):
        product = jnp.dot(
            factor, gt_ref[:, c * CHUNK : (c + 1) * CHUNK], preferred_element_type=F32
        )
        for b in range(HALF):
            t = HALF * u + b
            keeps = mask_ref[pl.ds(2 * t + parity, 1), c * CHUNK : (c + 1) * CHUNK]
            for first, last in ((0, 128), (128, CHUNK)) if c == 0 else ((0, CHUNK),):
                cols = slice(c * CHUNK + first, c * CHUNK + last)
                part = product[b * B : b * B + B, first:last]
                keep = keeps[:, first:last]
                new = front_ref[t, parity, :, cols].astype(F32) - part * keep
                if cols.stop == 128:
                    new = jnp.where(owner & (lane < B), part, new)
                out_ref[b, 0, :, cols] = new.astype(BF16)


def update(front4, parts, columns, row_w, mask):
    whole = pl.BlockSpec(memory_space=VMEM)
    return pl.pallas_call(
        update_kernel,
        grid=(2, 2),
        out_shape=jax.ShapeDtypeStruct((PAIRS, 2, B, COLS), BF16),
        in_specs=[whole] * 8,
        out_specs=pl.BlockSpec((HALF, 1, B, COLS), lambda p, u: (u, p, 0, 0)),
        compiler_params=pltpu.CompilerParams(vmem_limit_bytes=20 << 20),
        cost_estimate=pl.CostEstimate(
            flops=2 * 3072 * 1536 * 256, bytes_accessed=4 * 3072 * 1536, transcendentals=0
        ),
    )(front4, *parts, columns, row_w, mask)


def body(front, diag_inverse, fill_pattern):
    front4 = front.reshape(PAIRS, 2, B, COLS)
    packed = pack(lax.slice(front, (0, 0), (front.shape[0], 128)).reshape(PAIRS, 2, B, 128))
    row_w, col_w, mask, stay = prepare(front4, diag_inverse, fill_pattern)
    spread = [lax.ppermute(packed, ALL, spread_perm(k)) for k in range(3)]
    own, first, second = choose(packed, *spread)
    g0 = lax.ppermute(first, ALL, column_perm(0))
    g1 = lax.ppermute(second, ALL, column_perm(1))
    z_next = lax.ppermute(own, "z", [((i + 1) % 4, i) for i in range(4)])
    z_prev = lax.ppermute(own, "z", [(i, (i + 1) % 4) for i in range(4)])
    y_pair = lax.ppermute(own, "y", [(1, 2), (2, 1), (3, 0), (0, 3)])
    swap = [(0, 1), (1, 0)]
    g2 = lax.ppermute(g0, "core", swap)
    g3 = lax.ppermute(g1, "core", swap)
    columns = column_factor((g0, g1, g2, g3), col_w)
    out = update(stay, (own, z_next, y_pair, z_prev), columns, row_w, mask)
    return out.reshape(front.shape)


def solution(mesh):
    fine = Mesh(mesh.devices.reshape(4, 2, 4, 4), ALL)
    spec = P(("x", "core"), ("y", "z"))
    return jax.shard_map(
        body,
        mesh=fine,
        in_specs=(spec, P(), P()),
        out_specs=spec,
        check_vma=False,
    )
```

```python
import jax
import jax.numpy as jnp
from jax import lax
from jax.experimental import pallas as pl
from jax.experimental.pallas import tpu as pltpu
from jax.sharding import Mesh, PartitionSpec as P

BF16 = jnp.bfloat16
F32 = jnp.float32
B = 64
Q = 4
BLOCKS = 48
PAIRS = 24
HALF = 12
ROWS = HALF * B
COLS = 1536
WIDTH = 256
ALL = ("x", "core", "y", "z")
VMEM = pltpu.VMEM
NT = (((1,), (1,)), ((), ()))


def linear(x, core, y, z):
    return ((x * 2 + core) * 4 + y) * 4 + z


def quarter_of(y, z):
    return (z + 2 * (y // 2)) % 4


def spread_perm(step):
    pairs = []
    for x in range(4):
        for core in range(2):
            for j in range(4):
                target = [(1, j), (2, (j + 2) % 4), (3, (j + 2) % 4)][step]
                pairs.append((linear(x, core, 0, j), linear(x, core, *target)))
    return pairs


def column_perm(step):
    pairs = []
    for x in range(4):
        for core in range(2):
            r = 2 * x + core
            for y in range(4):
                for z in range(4):
                    q, half, far = quarter_of(y, z), y % 2, y // 2
                    near = (step == 0) == (q < 2)
                    to_x = (x + far + (0 if near else 2)) % 4
                    target = linear(to_x, q % 2, 2 * half + r // 4, r % 4)
                    pairs.append((linear(x, core, y, z), target))
    return pairs


def shift_perm(first, second):
    pairs = []
    for x in range(4):
        for core in range(2):
            dy, dz = (first, second)[core]
            for y in range(4):
                for z in range(4):
                    source = linear(x, core, (y + dy) % 4, (z + dz) % 4)
                    pairs.append((source, linear(x, core, y, z)))
    return pairs


OFFSETS = (
    ((0, 1), (0, 1)),
    ((2, 0), (0, 2)),
    ((0, -1), (0, -1)),
    ((1, 0), (1, 0)),
    ((-1, -1), (-1, -1)),
    ((-1, 0), (-1, 0)),
    ((-1, 1), (1, -1)),
)


def pack_kernel(panel_ref, even_ref, odd_ref):
    for parity, ref in enumerate((even_ref, odd_ref)):
        left = panel_ref[:HALF, parity, :, :].reshape(ROWS, 128)
        right = panel_ref[HALF:, parity, :, :].reshape(ROWS, 128)
        ref[...] = jnp.concatenate([left[:, :B], right[:, :B]], axis=1)


def pack(panel4):
    whole = pl.BlockSpec(memory_space=VMEM)
    return pl.pallas_call(
        pack_kernel,
        out_shape=(jax.ShapeDtypeStruct((ROWS, 128), BF16),) * 2,
        in_specs=[whole],
        out_specs=(whole,) * 2,
        compiler_params=pltpu.CompilerParams(vmem_limit_bytes=16 << 20),
    )(panel4)


def choose_kernel(a_ref, b_ref, c_ref, d_ref, own_ref):
    y = lax.axis_index("y")
    for k, ref in enumerate((a_ref, b_ref, c_ref, d_ref)):

        @pl.when(y == k)
        def _():
            own_ref[...] = ref[...]


def choose(a, b, c, d):
    whole = pl.BlockSpec(memory_space=VMEM)
    return pl.pallas_call(
        choose_kernel,
        out_shape=jax.ShapeDtypeStruct((ROWS, 128), BF16),
        in_specs=[whole] * 4,
        out_specs=whole,
        compiler_params=pltpu.CompilerParams(vmem_limit_bytes=16 << 20),
    )(a, b, c, d)


STAGES = 4


def prepare_kernel(
    front_ref, diag_ref, pattern_ref, row_w_ref, col_w_ref, mask_ref, stay_ref, sems
):
    span = PAIRS // STAGES
    copies = []
    for k in range(STAGES):
        part = pl.ds(k * span, span)
        copies.append(
            pltpu.make_async_copy(front_ref.at[part], stay_ref.at[part], sems.at[k])
        )
        copies[-1].start()
    x, core = lax.axis_index("x"), lax.axis_index("core")
    y, z = lax.axis_index("y"), lax.axis_index("z")
    own = lax.rem(z + 2 * (y // 2), 4)
    diag = diag_ref[...]
    eye = (
        lax.broadcasted_iota(jnp.int32, (WIDTH, WIDTH), 0)
        == lax.broadcasted_iota(jnp.int32, (WIDTH, WIDTH), 1)
    ).astype(BF16)
    turned = lax.dot_general(eye, diag, NT, preferred_element_type=F32).astype(BF16)
    bases = (own, lax.rem(own + 2 * lax.rem(y, 2), 4))
    source_x = 2 * lax.rem(y, 2) + z // 2
    half = lax.rem(x - source_x + 4, 4) // 2
    for q in range(Q):
        part = turned[q * B : q * B + B, :]
        zero = jnp.zeros_like(part)
        for kind, base in enumerate(bases):
            slot = lax.rem(q - base + 4, 4)
            row_w_ref[kind, 0, slot] = jnp.concatenate([part, zero], axis=0)
            row_w_ref[kind, 1, slot] = jnp.concatenate([zero, part], axis=0)
        other = jnp.where(q % 2 == core, 0, 2)
        late = jnp.where(q // 2 == half, 0, 1)
        part = diag[:, q * B : q * B + B]
        zero = jnp.zeros_like(part)
        col_w_ref[0, other + late] = jnp.concatenate([part, zero], axis=1)
        col_w_ref[1, other + late] = jnp.concatenate([zero, part], axis=1)
    row_id = x * 2 + core
    col_id = y * 4 + z
    count = pattern_ref.shape[0]
    rows = (
        lax.broadcasted_iota(jnp.int32, (BLOCKS, count), 0) * 8 + row_id
        == lax.broadcasted_iota(jnp.int32, (BLOCKS, count), 1)
    ).astype(BF16)
    cols = (
        lax.broadcasted_iota(jnp.int32, (count, COLS), 0)
        == lax.broadcasted_iota(jnp.int32, (count, COLS), 1) // B * 16 + col_id
    ).astype(BF16)
    picked = jnp.dot(
        rows, pattern_ref[...].astype(F32).astype(BF16), preferred_element_type=F32
    ).astype(BF16)
    keep = jnp.dot(picked, cols, preferred_element_type=F32)
    stored_row = lax.broadcasted_iota(jnp.int32, (BLOCKS, COLS), 0)
    stored_col = lax.broadcasted_iota(jnp.int32, (BLOCKS, COLS), 1) // B
    inside = (stored_row * 8 + row_id >= Q) & (stored_col * 16 + col_id >= Q)
    mask_ref[...] = jnp.where(inside, keep, 0.0)
    for copy in copies:
        copy.wait()


def prepare(front4, diag_inverse, fill_pattern):
    whole = pl.BlockSpec(memory_space=VMEM)
    return pl.pallas_call(
        prepare_kernel,
        out_shape=(
            jax.ShapeDtypeStruct((2, 2, Q, 128, WIDTH), BF16),
            jax.ShapeDtypeStruct((2, Q, WIDTH, 128), BF16),
            jax.ShapeDtypeStruct((BLOCKS, COLS), F32),
            jax.ShapeDtypeStruct(front4.shape, BF16),
        ),
        in_specs=[pl.BlockSpec(memory_space=pltpu.HBM), whole, whole],
        out_specs=(whole,) * 4,
        scratch_shapes=[pltpu.SemaphoreType.DMA((STAGES,))],
        compiler_params=pltpu.CompilerParams(vmem_limit_bytes=41 << 20),
        cost_estimate=pl.CostEstimate(
            flops=0, bytes_accessed=2 * 3072 * 1536 * 2, transcendentals=0
        ),
    )(front4, diag_inverse, fill_pattern)


def column_kernel(g0, g1, g2, g3, col_w_ref, out_ref):
    col_id = lax.axis_index("y") * 4 + lax.axis_index("z")
    for u in range(2):
        total = jnp.zeros((WIDTH, ROWS), F32)
        for k, g in enumerate((g0, g1, g2, g3)):
            total += lax.dot_general(col_w_ref[u, k], g[...], NT, preferred_element_type=F32)
        out_ref[:, u * ROWS : (u + 1) * ROWS] = total.astype(BF16)

    @pl.when(col_id < Q)
    def _():
        lane = lax.broadcasted_iota(jnp.int32, (WIDTH, 128), 1)
        line = lax.broadcasted_iota(jnp.int32, (WIDTH, 128), 0)
        pick = (line == lane + col_id * B).astype(F32)
        old = out_ref[:, :128].astype(F32)
        out_ref[:, :128] = jnp.where(lane < B, pick, old).astype(BF16)


def column_factor(columns, col_w):
    whole = pl.BlockSpec(memory_space=VMEM)
    return pl.pallas_call(
        column_kernel,
        out_shape=jax.ShapeDtypeStruct((WIDTH, COLS), BF16),
        in_specs=[whole] * 5,
        out_specs=whole,
        compiler_params=pltpu.CompilerParams(vmem_limit_bytes=16 << 20),
        cost_estimate=pl.CostEstimate(
            flops=2 * COLS * 256 * 512, bytes_accessed=2 * COLS * 768, transcendentals=0
        ),
    )(*columns, col_w)


CHUNK = 512


def update_kernel(front_ref, *refs):
    parts, (gt_ref, row_w_ref, mask_ref, out_ref, factor_ref) = refs[:8], refs[8:]
    parity, u = pl.program_id(0), pl.program_id(1)
    y, z = lax.axis_index("y"), lax.axis_index("z")
    owner = y * 4 + z < Q
    for kind in range(2):

        @pl.when(lax.rem(y + kind, 2) == parity)
        def _():
            four = [p[...] for p in parts[4 * kind : 4 * kind + 4]]
            factor_ref[...] = jnp.dot(
                jnp.concatenate(four, axis=1),
                row_w_ref[kind, u].reshape(Q * 128, WIDTH),
                preferred_element_type=F32,
            ).astype(BF16)

    factor = factor_ref[...]
    lane = lax.broadcasted_iota(jnp.int32, (B, 128), 1)
    for c in range(COLS // CHUNK):
        product = jnp.dot(
            factor, gt_ref[:, c * CHUNK : (c + 1) * CHUNK], preferred_element_type=F32
        )
        for b in range(HALF):
            t = HALF * u + b
            keeps = mask_ref[pl.ds(2 * t + parity, 1), c * CHUNK : (c + 1) * CHUNK]
            for first, last in ((0, 128), (128, CHUNK)) if c == 0 else ((0, CHUNK),):
                cols = slice(c * CHUNK + first, c * CHUNK + last)
                part = product[b * B : b * B + B, first:last]
                keep = keeps[:, first:last]
                new = front_ref[t, parity, :, cols].astype(F32) - part * keep
                if cols.stop == 128:
                    new = jnp.where(owner & (lane < B), part, new)
                out_ref[b, 0, :, cols] = new.astype(BF16)


def update(front4, parts, columns, row_w, mask):
    whole = pl.BlockSpec(memory_space=VMEM)
    return pl.pallas_call(
        update_kernel,
        grid=(2, 2),
        out_shape=jax.ShapeDtypeStruct((PAIRS, 2, B, COLS), BF16),
        in_specs=[whole] * 12,
        scratch_shapes=[VMEM((ROWS, WIDTH), BF16)],
        out_specs=pl.BlockSpec((HALF, 1, B, COLS), lambda p, u: (u, p, 0, 0)),
        compiler_params=pltpu.CompilerParams(vmem_limit_bytes=20 << 20),
        cost_estimate=pl.CostEstimate(
            flops=2 * 3072 * 1536 * 256, bytes_accessed=4 * 3072 * 1536, transcendentals=0
        ),
    )(front4, *parts, columns, row_w, mask)


def body(front, diag_inverse, fill_pattern):
    front4 = front.reshape(PAIRS, 2, B, COLS)
    even, odd = pack(lax.slice(front, (0, 0), (front.shape[0], 128)).reshape(PAIRS, 2, B, 128))
    row_w, col_w, mask, stay = prepare(front4, diag_inverse, fill_pattern)
    spread = [
        lax.ppermute(part, ALL, spread_perm(k)) for k, part in enumerate((odd, even, odd))
    ]
    own = choose(even, *spread)
    g0 = lax.ppermute(own, ALL, column_perm(0))
    g1 = lax.ppermute(own, ALL, column_perm(1))
    parts = [own] + [lax.ppermute(own, ALL, shift_perm(*offsets)) for offsets in OFFSETS]
    swap = [(0, 1), (1, 0)]
    g2 = lax.ppermute(g0, "core", swap)
    g3 = lax.ppermute(g1, "core", swap)
    columns = column_factor((g0, g1, g2, g3), col_w)
    out = update(stay, parts, columns, row_w, mask)
    return out.reshape(front.shape)


def solution(mesh):
    fine = Mesh(mesh.devices.reshape(4, 2, 4, 4), ALL)
    spec = P(("x", "core"), ("y", "z"))
    return jax.shard_map(
        body,
        mesh=fine,
        in_specs=(spec, P(), P()),
        out_specs=spec,
        check_vma=False,
    )
```

```python
import jax
import jax.numpy as jnp
from jax import lax
from jax.experimental import pallas as pl
from jax.experimental.pallas import tpu as pltpu
from jax.sharding import Mesh, PartitionSpec as P

BF16 = jnp.bfloat16
F32 = jnp.float32
B = 64
Q = 4
BLOCKS = 48
PAIRS = 24
HALF = 12
ROWS = HALF * B
COLS = 1536
WIDTH = 256
ALL = ("x", "core", "y", "z")
VMEM = pltpu.VMEM
NT = (((1,), (1,)), ((), ()))


def linear(x, core, y, z):
    return ((x * 2 + core) * 4 + y) * 4 + z


def quarter_of(y, z):
    return (z + 2 * (y // 2)) % 4


def spread_perm(step):
    pairs = []
    for x in range(4):
        for core in range(2):
            for j in range(4):
                target = [(1, j), (2, (j + 2) % 4), (3, (j + 2) % 4)][step]
                pairs.append((linear(x, core, 0, j), linear(x, core, *target)))
    return pairs


def column_perm(step):
    pairs = []
    for x in range(4):
        for core in range(2):
            r = 2 * x + core
            for y in range(4):
                for z in range(4):
                    q, half, far = quarter_of(y, z), y % 2, y // 2
                    near = (step == 0) == (q < 2)
                    to_x = (x + far + (0 if near else 2)) % 4
                    target = linear(to_x, q % 2, 2 * half + r // 4, r % 4)
                    pairs.append((linear(x, core, y, z), target))
    return pairs


def shift_perm(first, second):
    pairs = []
    for x in range(4):
        for core in range(2):
            dy, dz = (first, second)[core]
            for y in range(4):
                for z in range(4):
                    source = linear(x, core, (y + dy) % 4, (z + dz) % 4)
                    pairs.append((source, linear(x, core, y, z)))
    return pairs


OFFSETS = (
    ((0, 1), (0, 1)),
    ((2, 0), (0, 2)),
    ((0, -1), (0, -1)),
    ((1, 0), (1, 0)),
    ((1, 1), (1, 1)),
    ((-1, 0), (-1, 0)),
    ((1, -1), (-1, 1)),
)


def pack_kernel(panel_ref, even_ref, odd_ref):
    for parity, ref in enumerate((even_ref, odd_ref)):
        left = panel_ref[:HALF, parity, :, :].reshape(ROWS, 128)
        right = panel_ref[HALF:, parity, :, :].reshape(ROWS, 128)
        ref[...] = jnp.concatenate([left[:, :B], right[:, :B]], axis=1)


def pack(panel4):
    whole = pl.BlockSpec(memory_space=VMEM)
    return pl.pallas_call(
        pack_kernel,
        out_shape=(jax.ShapeDtypeStruct((ROWS, 128), BF16),) * 2,
        in_specs=[whole],
        out_specs=(whole,) * 2,
        compiler_params=pltpu.CompilerParams(vmem_limit_bytes=16 << 20),
    )(panel4)


def choose_kernel(a_ref, b_ref, c_ref, d_ref, own_ref):
    y = lax.axis_index("y")
    for k, ref in enumerate((a_ref, b_ref, c_ref, d_ref)):

        @pl.when(y == k)
        def _():
            own_ref[...] = ref[...]


def choose(a, b, c, d):
    whole = pl.BlockSpec(memory_space=VMEM)
    return pl.pallas_call(
        choose_kernel,
        out_shape=jax.ShapeDtypeStruct((ROWS, 128), BF16),
        in_specs=[whole] * 4,
        out_specs=whole,
        compiler_params=pltpu.CompilerParams(vmem_limit_bytes=16 << 20),
    )(a, b, c, d)


STAGES = 4


def prepare_kernel(
    front_ref, diag_ref, pattern_ref, row_w_ref, col_w_ref, mask_ref, stay_ref, sems
):
    span = PAIRS // STAGES
    copies = []
    for k in range(STAGES):
        part = pl.ds(k * span, span)
        copies.append(
            pltpu.make_async_copy(front_ref.at[part], stay_ref.at[part], sems.at[k])
        )
        copies[-1].start()
    x, core = lax.axis_index("x"), lax.axis_index("core")
    y, z = lax.axis_index("y"), lax.axis_index("z")
    own = lax.rem(z + 2 * (y // 2), 4)
    diag = diag_ref[...]
    eye = (
        lax.broadcasted_iota(jnp.int32, (WIDTH, WIDTH), 0)
        == lax.broadcasted_iota(jnp.int32, (WIDTH, WIDTH), 1)
    ).astype(BF16)
    turned = lax.dot_general(eye, diag, NT, preferred_element_type=F32).astype(BF16)
    bases = (own, lax.rem(own + 2 * lax.rem(y, 2), 4))
    source_x = 2 * lax.rem(y, 2) + z // 2
    half = lax.rem(x - source_x + 4, 4) // 2
    for q in range(Q):
        part = turned[q * B : q * B + B, :]
        zero = jnp.zeros_like(part)
        for kind, base in enumerate(bases):
            slot = lax.rem(q - base + 4, 4)
            row_w_ref[kind, 0, slot] = jnp.concatenate([part, zero], axis=0)
            row_w_ref[kind, 1, slot] = jnp.concatenate([zero, part], axis=0)
        other = jnp.where(q % 2 == core, 0, 2)
        late = jnp.where(q // 2 == half, 0, 1)
        part = diag[:, q * B : q * B + B]
        zero = jnp.zeros_like(part)
        col_w_ref[0, other + late] = jnp.concatenate([part, zero], axis=1)
        col_w_ref[1, other + late] = jnp.concatenate([zero, part], axis=1)
    row_id = x * 2 + core
    col_id = y * 4 + z
    count = pattern_ref.shape[0]
    rows = (
        lax.broadcasted_iota(jnp.int32, (BLOCKS, count), 0) * 8 + row_id
        == lax.broadcasted_iota(jnp.int32, (BLOCKS, count), 1)
    ).astype(BF16)
    cols = (
        lax.broadcasted_iota(jnp.int32, (count, COLS), 0)
        == lax.broadcasted_iota(jnp.int32, (count, COLS), 1) // B * 16 + col_id
    ).astype(BF16)
    picked = jnp.dot(
        rows, pattern_ref[...].astype(F32).astype(BF16), preferred_element_type=F32
    ).astype(BF16)
    keep = jnp.dot(picked, cols, preferred_element_type=F32)
    stored_row = lax.broadcasted_iota(jnp.int32, (BLOCKS, COLS), 0)
    stored_col = lax.broadcasted_iota(jnp.int32, (BLOCKS, COLS), 1) // B
    inside = (stored_row * 8 + row_id >= Q) & (stored_col * 16 + col_id >= Q)
    mask_ref[...] = jnp.where(inside, keep, 0.0)
    for copy in copies:
        copy.wait()


def prepare(front4, diag_inverse, fill_pattern):
    whole = pl.BlockSpec(memory_space=VMEM)
    return pl.pallas_call(
        prepare_kernel,
        out_shape=(
            jax.ShapeDtypeStruct((2, 2, Q, 128, WIDTH), BF16),
            jax.ShapeDtypeStruct((2, Q, WIDTH, 128), BF16),
            jax.ShapeDtypeStruct((BLOCKS, COLS), F32),
            jax.ShapeDtypeStruct(front4.shape, BF16),
        ),
        in_specs=[pl.BlockSpec(memory_space=pltpu.HBM), whole, whole],
        out_specs=(whole,) * 4,
        scratch_shapes=[pltpu.SemaphoreType.DMA((STAGES,))],
        compiler_params=pltpu.CompilerParams(vmem_limit_bytes=41 << 20),
        cost_estimate=pl.CostEstimate(
            flops=0, bytes_accessed=2 * 3072 * 1536 * 2, transcendentals=0
        ),
    )(front4, diag_inverse, fill_pattern)


def column_kernel(g0, g1, g2, g3, col_w_ref, out_ref):
    col_id = lax.axis_index("y") * 4 + lax.axis_index("z")
    for u in range(2):
        total = jnp.zeros((WIDTH, ROWS), F32)
        for k, g in enumerate((g0, g1, g2, g3)):
            total += lax.dot_general(col_w_ref[u, k], g[...], NT, preferred_element_type=F32)
        out_ref[:, u * ROWS : (u + 1) * ROWS] = total.astype(BF16)

    @pl.when(col_id < Q)
    def _():
        lane = lax.broadcasted_iota(jnp.int32, (WIDTH, 128), 1)
        line = lax.broadcasted_iota(jnp.int32, (WIDTH, 128), 0)
        pick = (line == lane + col_id * B).astype(F32)
        old = out_ref[:, :128].astype(F32)
        out_ref[:, :128] = jnp.where(lane < B, pick, old).astype(BF16)


def column_factor(columns, col_w):
    whole = pl.BlockSpec(memory_space=VMEM)
    return pl.pallas_call(
        column_kernel,
        out_shape=jax.ShapeDtypeStruct((WIDTH, COLS), BF16),
        in_specs=[whole] * 5,
        out_specs=whole,
        compiler_params=pltpu.CompilerParams(vmem_limit_bytes=16 << 20),
        cost_estimate=pl.CostEstimate(
            flops=2 * COLS * 256 * 512, bytes_accessed=2 * COLS * 768, transcendentals=0
        ),
    )(*columns, col_w)


CHUNK = 512


def update_kernel(front_ref, *refs):
    parts, (gt_ref, row_w_ref, mask_ref, out_ref, factor_ref) = refs[:8], refs[8:]
    parity, u = pl.program_id(0), pl.program_id(1)
    y, z = lax.axis_index("y"), lax.axis_index("z")
    owner = y * 4 + z < Q
    for kind in range(2):

        @pl.when(lax.rem(y + kind, 2) == parity)
        def _():
            four = [p[...] for p in parts[4 * kind : 4 * kind + 4]]
            factor_ref[...] = jnp.dot(
                jnp.concatenate(four, axis=1),
                row_w_ref[kind, u].reshape(Q * 128, WIDTH),
                preferred_element_type=F32,
            ).astype(BF16)

    factor = factor_ref[...]
    lane = lax.broadcasted_iota(jnp.int32, (B, 128), 1)
    for c in range(COLS // CHUNK):
        product = jnp.dot(
            factor, gt_ref[:, c * CHUNK : (c + 1) * CHUNK], preferred_element_type=F32
        )
        for b in range(HALF):
            t = HALF * u + b
            keeps = mask_ref[pl.ds(2 * t + parity, 1), c * CHUNK : (c + 1) * CHUNK]
            for first, last in ((0, 128), (128, CHUNK)) if c == 0 else ((0, CHUNK),):
                cols = slice(c * CHUNK + first, c * CHUNK + last)
                part = product[b * B : b * B + B, first:last]
                keep = keeps[:, first:last]
                new = front_ref[t, parity, :, cols].astype(F32) - part * keep
                if cols.stop == 128:
                    new = jnp.where(owner & (lane < B), part, new)
                out_ref[b, 0, :, cols] = new.astype(BF16)


def update(front4, parts, columns, row_w, mask):
    whole = pl.BlockSpec(memory_space=VMEM)
    return pl.pallas_call(
        update_kernel,
        grid=(2, 2),
        out_shape=jax.ShapeDtypeStruct((PAIRS, 2, B, COLS), BF16),
        in_specs=[whole] * 12,
        scratch_shapes=[VMEM((ROWS, WIDTH), BF16)],
        out_specs=pl.BlockSpec((HALF, 1, B, COLS), lambda p, u: (u, p, 0, 0)),
        compiler_params=pltpu.CompilerParams(vmem_limit_bytes=20 << 20),
        cost_estimate=pl.CostEstimate(
            flops=2 * 3072 * 1536 * 256, bytes_accessed=4 * 3072 * 1536, transcendentals=0
        ),
    )(front4, *parts, columns, row_w, mask)


def body(front, diag_inverse, fill_pattern):
    front4 = front.reshape(PAIRS, 2, B, COLS)
    even, odd = pack(lax.slice(front, (0, 0), (front.shape[0], 128)).reshape(PAIRS, 2, B, 128))
    row_w, col_w, mask, stay = prepare(front4, diag_inverse, fill_pattern)
    spread = [
        lax.ppermute(part, ALL, spread_perm(k)) for k, part in enumerate((odd, even, odd))
    ]
    own = choose(even, *spread)
    g0 = lax.ppermute(own, ALL, column_perm(0))
    g1 = lax.ppermute(own, ALL, column_perm(1))
    parts = [own] + [lax.ppermute(own, ALL, shift_perm(*offsets)) for offsets in OFFSETS]
    swap = [(0, 1), (1, 0)]
    g2 = lax.ppermute(g0, "core", swap)
    g3 = lax.ppermute(g1, "core", swap)
    columns = column_factor((g0, g1, g2, g3), col_w)
    out = update(stay, parts, columns, row_w, mask)
    return out.reshape(front.shape)


def solution(mesh):
    fine = Mesh(mesh.devices.reshape(4, 2, 4, 4), ALL)
    spec = P(("x", "core"), ("y", "z"))
    return jax.shard_map(
        body,
        mesh=fine,
        in_specs=(spec, P(), P()),
        out_specs=spec,
        check_vma=False,
    )
```

```python
import jax
import jax.numpy as jnp
from jax import lax
from jax.experimental import pallas as pl
from jax.experimental.pallas import tpu as pltpu
from jax.sharding import Mesh, PartitionSpec as P

BF16 = jnp.bfloat16
F32 = jnp.float32
B = 64
Q = 4
BLOCKS = 48
PAIRS = 24
HALF = 12
ROWS = HALF * B
COLS = 1536
WIDTH = 256
ALL = ("x", "core", "y", "z")
VMEM = pltpu.VMEM
NT = (((1,), (1,)), ((), ()))


def linear(x, core, y, z):
    return ((x * 2 + core) * 4 + y) * 4 + z


def quarter_of(y, z):
    return (z + 2 * (y // 2)) % 4


def spread_perm(step):
    pairs = []
    for x in range(4):
        for core in range(2):
            for j in range(4):
                target = [(1, j), (2, (j + 2) % 4), (3, (j + 2) % 4)][step]
                pairs.append((linear(x, core, 0, j), linear(x, core, *target)))
    return pairs


def column_perm():
    pairs = []
    for x in range(4):
        for core in range(2):
            r = 2 * x + core
            for y in range(4):
                for z in range(4):
                    to_x = (x + 2 * (y // 2) + z % 2) % 4
                    target = linear(to_x, quarter_of(y, z) // 2, 2 * (y % 2) + r // 4, r % 4)
                    pairs.append((linear(x, core, y, z), target))
    return pairs


def pack_kernel(panel_ref, even_ref, odd_ref):
    for parity, ref in enumerate((even_ref, odd_ref)):
        left = panel_ref[:HALF, parity, :, :].reshape(ROWS, 128)
        right = panel_ref[HALF:, parity, :, :].reshape(ROWS, 128)
        ref[...] = jnp.concatenate([left[:, :B], right[:, :B]], axis=1)


def pack(panel4):
    whole = pl.BlockSpec(memory_space=VMEM)
    return pl.pallas_call(
        pack_kernel,
        out_shape=(jax.ShapeDtypeStruct((ROWS, 128), BF16),) * 2,
        in_specs=[whole],
        out_specs=(whole,) * 2,
        compiler_params=pltpu.CompilerParams(vmem_limit_bytes=16 << 20),
    )(panel4)


def choose_kernel(a_ref, b_ref, c_ref, d_ref, own_ref):
    y = lax.axis_index("y")
    for k, ref in enumerate((a_ref, b_ref, c_ref, d_ref)):

        @pl.when(y == k)
        def _():
            own_ref[...] = ref[...]


def choose(a, b, c, d):
    whole = pl.BlockSpec(memory_space=VMEM)
    return pl.pallas_call(
        choose_kernel,
        out_shape=jax.ShapeDtypeStruct((ROWS, 128), BF16),
        in_specs=[whole] * 4,
        out_specs=whole,
        compiler_params=pltpu.CompilerParams(vmem_limit_bytes=16 << 20),
    )(a, b, c, d)


STAGES = 4


def prepare_kernel(
    front_ref, diag_ref, pattern_ref, row_w_ref, col_w_ref, mask_ref, stay_ref, sems
):
    span = PAIRS // STAGES
    copies = []
    for k in range(STAGES):
        part = pl.ds(k * span, span)
        copies.append(
            pltpu.make_async_copy(front_ref.at[part], stay_ref.at[part], sems.at[k])
        )
        copies[-1].start()
    x, core = lax.axis_index("x"), lax.axis_index("core")
    y, z = lax.axis_index("y"), lax.axis_index("z")
    own = lax.rem(z + 2 * (y // 2), 4)
    diag = diag_ref[...]
    eye = (
        lax.broadcasted_iota(jnp.int32, (WIDTH, WIDTH), 0)
        == lax.broadcasted_iota(jnp.int32, (WIDTH, WIDTH), 1)
    ).astype(BF16)
    turned = lax.dot_general(eye, diag, NT, preferred_element_type=F32).astype(BF16)
    bases = (own, lax.rem(own + 2 * lax.rem(y, 2), 4))
    source_x = 2 * lax.rem(y, 2) + z // 2
    swapped = lax.rem(x - source_x + 4, 2)
    for q in range(Q):
        part = turned[q * B : q * B + B, :]
        zero = jnp.zeros_like(part)
        for kind, base in enumerate(bases):
            slot = jnp.bitwise_xor(q, base)
            row_w_ref[kind, 0, slot] = jnp.concatenate([part, zero], axis=0)
            row_w_ref[kind, 1, slot] = jnp.concatenate([zero, part], axis=0)
        other = jnp.where(q // 2 == core, 0, 2)
        late = jnp.bitwise_xor(q % 2, swapped)
        part = diag[:, q * B : q * B + B]
        zero = jnp.zeros_like(part)
        col_w_ref[0, other + late] = jnp.concatenate([part, zero], axis=1)
        col_w_ref[1, other + late] = jnp.concatenate([zero, part], axis=1)
    row_id = x * 2 + core
    col_id = y * 4 + z
    count = pattern_ref.shape[0]
    rows = (
        lax.broadcasted_iota(jnp.int32, (BLOCKS, count), 0) * 8 + row_id
        == lax.broadcasted_iota(jnp.int32, (BLOCKS, count), 1)
    ).astype(BF16)
    cols = (
        lax.broadcasted_iota(jnp.int32, (count, COLS), 0)
        == lax.broadcasted_iota(jnp.int32, (count, COLS), 1) // B * 16 + col_id
    ).astype(BF16)
    picked = jnp.dot(
        rows, pattern_ref[...].astype(F32).astype(BF16), preferred_element_type=F32
    ).astype(BF16)
    keep = jnp.dot(picked, cols, preferred_element_type=F32)
    stored_row = lax.broadcasted_iota(jnp.int32, (BLOCKS, COLS), 0)
    stored_col = lax.broadcasted_iota(jnp.int32, (BLOCKS, COLS), 1) // B
    inside = (stored_row * 8 + row_id >= Q) & (stored_col * 16 + col_id >= Q)
    mask_ref[...] = jnp.where(inside, keep, 0.0)
    for copy in copies:
        copy.wait()


def prepare(front4, diag_inverse, fill_pattern):
    whole = pl.BlockSpec(memory_space=VMEM)
    return pl.pallas_call(
        prepare_kernel,
        out_shape=(
            jax.ShapeDtypeStruct((2, 2, Q, 128, WIDTH), BF16),
            jax.ShapeDtypeStruct((2, Q, WIDTH, 128), BF16),
            jax.ShapeDtypeStruct((BLOCKS, COLS), F32),
            jax.ShapeDtypeStruct(front4.shape, BF16),
        ),
        in_specs=[pl.BlockSpec(memory_space=pltpu.HBM), whole, whole],
        out_specs=(whole,) * 4,
        scratch_shapes=[pltpu.SemaphoreType.DMA((STAGES,))],
        compiler_params=pltpu.CompilerParams(vmem_limit_bytes=41 << 20),
        cost_estimate=pl.CostEstimate(
            flops=0, bytes_accessed=2 * 3072 * 1536 * 2, transcendentals=0
        ),
    )(front4, diag_inverse, fill_pattern)


def column_kernel(near_ref, far_ref, col_w_ref, out_ref):
    col_id = lax.axis_index("y") * 4 + lax.axis_index("z")
    for u in range(2):
        total = jnp.zeros((WIDTH, ROWS), F32)
        for k in range(Q):
            g = (near_ref, far_ref)[k // 2][k % 2]
            total += lax.dot_general(col_w_ref[u, k], g, NT, preferred_element_type=F32)
        out_ref[:, u * ROWS : (u + 1) * ROWS] = total.astype(BF16)

    @pl.when(col_id < Q)
    def _():
        lane = lax.broadcasted_iota(jnp.int32, (WIDTH, 128), 1)
        line = lax.broadcasted_iota(jnp.int32, (WIDTH, 128), 0)
        pick = (line == lane + col_id * B).astype(F32)
        old = out_ref[:, :128].astype(F32)
        out_ref[:, :128] = jnp.where(lane < B, pick, old).astype(BF16)


def column_factor(columns, col_w):
    whole = pl.BlockSpec(memory_space=VMEM)
    return pl.pallas_call(
        column_kernel,
        out_shape=jax.ShapeDtypeStruct((WIDTH, COLS), BF16),
        in_specs=[whole] * 3,
        out_specs=whole,
        compiler_params=pltpu.CompilerParams(vmem_limit_bytes=16 << 20),
        cost_estimate=pl.CostEstimate(
            flops=2 * COLS * 256 * 512, bytes_accessed=2 * COLS * 768, transcendentals=0
        ),
    )(*columns, col_w)


CHUNK = 512


def factor_kernel(own_ref, z_ref, next_ref, prev_ref, row_w_ref, out_ref):
    y = lax.axis_index("y")
    fours = (
        (own_ref[0], own_ref[1], z_ref[1], z_ref[0]),
        (next_ref[0], next_ref[1], prev_ref[0], prev_ref[1]),
    )
    for kind, four in enumerate(fours):
        parity = lax.rem(y + kind, 2)
        joined = jnp.concatenate(four, axis=1)
        for u in range(2):
            out_ref[parity, u] = jnp.dot(
                joined,
                row_w_ref[kind, u].reshape(Q * 128, WIDTH),
                preferred_element_type=F32,
            ).astype(BF16)


def row_factor(parts, row_w):
    whole = pl.BlockSpec(memory_space=VMEM)
    return pl.pallas_call(
        factor_kernel,
        out_shape=jax.ShapeDtypeStruct((2, 2, ROWS, WIDTH), BF16),
        in_specs=[whole] * 5,
        out_specs=whole,
        compiler_params=pltpu.CompilerParams(vmem_limit_bytes=16 << 20),
        cost_estimate=pl.CostEstimate(
            flops=2 * 3072 * 256 * 512, bytes_accessed=4 * 3072 * 256, transcendentals=0
        ),
    )(*parts, row_w)


def update_kernel(front_ref, factor_ref, gt_ref, mask_ref, out_ref):
    parity, u = pl.program_id(0), pl.program_id(1)
    owner = lax.axis_index("y") * 4 + lax.axis_index("z") < Q
    factor = factor_ref[parity, u]
    lane = lax.broadcasted_iota(jnp.int32, (B, 128), 1)
    for c in range(COLS // CHUNK):
        product = jnp.dot(
            factor, gt_ref[:, c * CHUNK : (c + 1) * CHUNK], preferred_element_type=F32
        )
        for b in range(HALF):
            t = HALF * u + b
            keeps = mask_ref[pl.ds(2 * t + parity, 1), c * CHUNK : (c + 1) * CHUNK]
            for first, last in ((0, 128), (128, CHUNK)) if c == 0 else ((0, CHUNK),):
                cols = slice(c * CHUNK + first, c * CHUNK + last)
                part = product[b * B : b * B + B, first:last]
                keep = keeps[:, first:last]
                new = front_ref[t, parity, :, cols].astype(F32) - part * keep
                if cols.stop == 128:
                    new = jnp.where(owner & (lane < B), part, new)
                out_ref[b, 0, :, cols] = new.astype(BF16)


def update(front4, factor, columns, mask):
    whole = pl.BlockSpec(memory_space=VMEM)
    return pl.pallas_call(
        update_kernel,
        grid=(2, 2),
        out_shape=jax.ShapeDtypeStruct((PAIRS, 2, B, COLS), BF16),
        in_specs=[whole] * 4,
        out_specs=pl.BlockSpec((HALF, 1, B, COLS), lambda p, u: (u, p, 0, 0)),
        compiler_params=pltpu.CompilerParams(vmem_limit_bytes=20 << 20),
        cost_estimate=pl.CostEstimate(
            flops=2 * 3072 * 1536 * 256, bytes_accessed=4 * 3072 * 1536, transcendentals=0
        ),
    )(front4, factor, columns, mask)


def body(front, diag_inverse, fill_pattern):
    front4 = front.reshape(PAIRS, 2, B, COLS)
    even, odd = pack(lax.slice(front, (0, 0), (front.shape[0], 128)).reshape(PAIRS, 2, B, 128))
    row_w, col_w, mask, stay = prepare(front4, diag_inverse, fill_pattern)
    spread = [
        lax.ppermute(part, ALL, spread_perm(k)) for k, part in enumerate((odd, even, odd))
    ]
    own = choose(even, *spread)
    mate = lax.ppermute(own, "z", [(0, 1), (1, 0), (2, 3), (3, 2)])
    pair = jnp.stack([own, mate])
    near = lax.ppermute(pair, ALL, column_perm())
    z_pair = lax.ppermute(pair, "z", [(1, 2), (2, 1), (3, 0), (0, 3)])
    y_next = lax.ppermute(pair, "y", [((i + 1) % 4, i) for i in range(4)])
    y_prev = lax.ppermute(pair, "y", [(i, (i + 1) % 4) for i in range(4)])
    far = lax.ppermute(near, "core", [(0, 1), (1, 0)])
    factor = row_factor((pair, z_pair, y_next, y_prev), row_w)
    columns = column_factor((near, far), col_w)
    out = update(stay, factor, columns, mask)
    return out.reshape(front.shape)


def solution(mesh):
    fine = Mesh(mesh.devices.reshape(4, 2, 4, 4), ALL)
    spec = P(("x", "core"), ("y", "z"))
    return jax.shard_map(
        body,
        mesh=fine,
        in_specs=(spec, P(), P()),
        out_specs=spec,
        check_vma=False,
    )
```

```python
import jax
import jax.numpy as jnp
from jax import lax
from jax.experimental import pallas as pl
from jax.experimental.pallas import tpu as pltpu
from jax.sharding import Mesh, PartitionSpec as P

BF16 = jnp.bfloat16
F32 = jnp.float32
B = 64
Q = 4
BLOCKS = 48
PAIRS = 24
HALF = 12
ROWS = HALF * B
COLS = 1536
WIDTH = 256
ALL = ("x", "core", "y", "z")
VMEM = pltpu.VMEM
NT = (((1,), (1,)), ((), ()))


def linear(x, core, y, z):
    return ((x * 2 + core) * 4 + y) * 4 + z


def quarter_of(y, z):
    return (z + 2 * (y // 2)) % 4


def spread_perm(step):
    pairs = []
    for x in range(4):
        for core in range(2):
            for j in range(4):
                target = [(1, j), (2, (j + 2) % 4), (3, (j + 2) % 4)][step]
                pairs.append((linear(x, core, 0, j), linear(x, core, *target)))
    return pairs


def column_perm():
    pairs = []
    for x in range(4):
        for core in range(2):
            r = 2 * x + core
            for y in range(4):
                for z in range(4):
                    to_x = (x + 2 * (y // 2) + z % 2) % 4
                    target = linear(to_x, quarter_of(y, z) // 2, 2 * (y % 2) + r // 4, r % 4)
                    pairs.append((linear(x, core, y, z), target))
    return pairs


def pack_kernel(panel_ref, even_ref, odd_ref):
    for parity, ref in enumerate((even_ref, odd_ref)):
        left = panel_ref[:HALF, parity, :, :].reshape(ROWS, 128)
        right = panel_ref[HALF:, parity, :, :].reshape(ROWS, 128)
        ref[...] = jnp.concatenate([left[:, :B], right[:, :B]], axis=1)


def pack(panel4):
    whole = pl.BlockSpec(memory_space=VMEM)
    return pl.pallas_call(
        pack_kernel,
        out_shape=(jax.ShapeDtypeStruct((ROWS, 128), BF16),) * 2,
        in_specs=[whole],
        out_specs=(whole,) * 2,
        compiler_params=pltpu.CompilerParams(vmem_limit_bytes=16 << 20),
    )(panel4)


def choose_kernel(a_ref, b_ref, c_ref, d_ref, own_ref):
    y = lax.axis_index("y")
    for k, ref in enumerate((a_ref, b_ref, c_ref, d_ref)):

        @pl.when(y == k)
        def _():
            own_ref[...] = ref[...]


def choose(a, b, c, d):
    whole = pl.BlockSpec(memory_space=VMEM)
    return pl.pallas_call(
        choose_kernel,
        out_shape=jax.ShapeDtypeStruct((ROWS, 128), BF16),
        in_specs=[whole] * 4,
        out_specs=whole,
        compiler_params=pltpu.CompilerParams(vmem_limit_bytes=16 << 20),
    )(a, b, c, d)


STAGES = 4


def prepare_kernel(
    front_ref, diag_ref, pattern_ref, row_w_ref, col_w_ref, mask_ref, stay_ref, sems
):
    span = PAIRS // STAGES
    copies = []
    for k in range(STAGES):
        part = pl.ds(k * span, span)
        copies.append(
            pltpu.make_async_copy(front_ref.at[part], stay_ref.at[part], sems.at[k])
        )
        copies[-1].start()
    x, core = lax.axis_index("x"), lax.axis_index("core")
    y, z = lax.axis_index("y"), lax.axis_index("z")
    own = lax.rem(z + 2 * (y // 2), 4)
    diag = diag_ref[...]
    eye = (
        lax.broadcasted_iota(jnp.int32, (WIDTH, WIDTH), 0)
        == lax.broadcasted_iota(jnp.int32, (WIDTH, WIDTH), 1)
    ).astype(BF16)
    turned = lax.dot_general(eye, diag, NT, preferred_element_type=F32).astype(BF16)
    bases = (own, lax.rem(own + 2 * lax.rem(y, 2), 4))
    source_x = 2 * lax.rem(y, 2) + z // 2
    swapped = lax.rem(x - source_x + 4, 2)
    for q in range(Q):
        part = turned[q * B : q * B + B, :]
        zero = jnp.zeros_like(part)
        for kind, base in enumerate(bases):
            slot = jnp.bitwise_xor(q, base)
            row_w_ref[kind, 0, slot] = jnp.concatenate([part, zero], axis=0)
            row_w_ref[kind, 1, slot] = jnp.concatenate([zero, part], axis=0)
        other = jnp.where(q // 2 == core, 0, 2)
        late = jnp.bitwise_xor(q % 2, swapped)
        part = diag[:, q * B : q * B + B]
        zero = jnp.zeros_like(part)
        col_w_ref[0, other + late] = jnp.concatenate([part, zero], axis=1)
        col_w_ref[1, other + late] = jnp.concatenate([zero, part], axis=1)
    row_id = x * 2 + core
    col_id = y * 4 + z
    count = pattern_ref.shape[0]
    rows = (
        lax.broadcasted_iota(jnp.int32, (BLOCKS, count), 0) * 8 + row_id
        == lax.broadcasted_iota(jnp.int32, (BLOCKS, count), 1)
    ).astype(BF16)
    cols = (
        lax.broadcasted_iota(jnp.int32, (count, COLS), 0)
        == lax.broadcasted_iota(jnp.int32, (count, COLS), 1) // B * 16 + col_id
    ).astype(BF16)
    picked = jnp.dot(
        rows, pattern_ref[...].astype(F32).astype(BF16), preferred_element_type=F32
    ).astype(BF16)
    keep = jnp.dot(picked, cols, preferred_element_type=F32)
    stored_row = lax.broadcasted_iota(jnp.int32, (BLOCKS, COLS), 0)
    stored_col = lax.broadcasted_iota(jnp.int32, (BLOCKS, COLS), 1) // B
    inside = (stored_row * 8 + row_id >= Q) & (stored_col * 16 + col_id >= Q)
    mask_ref[...] = jnp.where(inside, keep, 0.0)
    for copy in copies:
        copy.wait()


def prepare(front4, diag_inverse, fill_pattern):
    whole = pl.BlockSpec(memory_space=VMEM)
    return pl.pallas_call(
        prepare_kernel,
        out_shape=(
            jax.ShapeDtypeStruct((2, 2, Q, 128, WIDTH), BF16),
            jax.ShapeDtypeStruct((2, Q, WIDTH, 128), BF16),
            jax.ShapeDtypeStruct((BLOCKS, COLS), F32),
            jax.ShapeDtypeStruct(front4.shape, BF16),
        ),
        in_specs=[pl.BlockSpec(memory_space=pltpu.HBM), whole, whole],
        out_specs=(whole,) * 4,
        scratch_shapes=[pltpu.SemaphoreType.DMA((STAGES,))],
        compiler_params=pltpu.CompilerParams(vmem_limit_bytes=41 << 20),
        cost_estimate=pl.CostEstimate(
            flops=0, bytes_accessed=2 * 3072 * 1536 * 2, transcendentals=0
        ),
    )(front4, diag_inverse, fill_pattern)


def column_kernel(near_ref, far_ref, col_w_ref, out_ref):
    col_id = lax.axis_index("y") * 4 + lax.axis_index("z")
    for u in range(2):
        total = jnp.zeros((WIDTH, ROWS), F32)
        for k in range(Q):
            g = (near_ref, far_ref)[k // 2][k % 2]
            total += lax.dot_general(col_w_ref[u, k], g, NT, preferred_element_type=F32)
        out_ref[:, u * ROWS : (u + 1) * ROWS] = total.astype(BF16)

    @pl.when(col_id < Q)
    def _():
        lane = lax.broadcasted_iota(jnp.int32, (WIDTH, 128), 1)
        line = lax.broadcasted_iota(jnp.int32, (WIDTH, 128), 0)
        pick = (line == lane + col_id * B).astype(F32)
        old = out_ref[:, :128].astype(F32)
        out_ref[:, :128] = jnp.where(lane < B, pick, old).astype(BF16)


def column_factor(columns, col_w):
    whole = pl.BlockSpec(memory_space=VMEM)
    return pl.pallas_call(
        column_kernel,
        out_shape=jax.ShapeDtypeStruct((WIDTH, COLS), BF16),
        in_specs=[whole] * 3,
        out_specs=whole,
        compiler_params=pltpu.CompilerParams(vmem_limit_bytes=16 << 20),
        cost_estimate=pl.CostEstimate(
            flops=2 * COLS * 256 * 512, bytes_accessed=2 * COLS * 768, transcendentals=0
        ),
    )(*columns, col_w)


CHUNK = 512


def factor_kernel(own_ref, z_ref, next_ref, prev_ref, row_w_ref, out_ref):
    y = lax.axis_index("y")
    fours = (
        (own_ref[0], own_ref[1], z_ref[1], z_ref[0]),
        (next_ref[0], next_ref[1], prev_ref[0], prev_ref[1]),
    )
    for kind, four in enumerate(fours):
        parity = lax.rem(y + kind, 2)
        joined = jnp.concatenate(four, axis=1)
        for u in range(2):
            out_ref[parity, u] = jnp.dot(
                joined,
                row_w_ref[kind, u].reshape(Q * 128, WIDTH),
                preferred_element_type=F32,
            ).astype(BF16)


def row_factor(parts, row_w):
    whole = pl.BlockSpec(memory_space=VMEM)
    return pl.pallas_call(
        factor_kernel,
        out_shape=jax.ShapeDtypeStruct((2, 2, ROWS, WIDTH), BF16),
        in_specs=[whole] * 5,
        out_specs=whole,
        compiler_params=pltpu.CompilerParams(vmem_limit_bytes=16 << 20),
        cost_estimate=pl.CostEstimate(
            flops=2 * 3072 * 256 * 512, bytes_accessed=4 * 3072 * 256, transcendentals=0
        ),
    )(*parts, row_w)


def update_kernel(front_ref, factor_ref, gt_ref, mask_ref, out_ref):
    parity, u = pl.program_id(0), pl.program_id(1)
    owner = lax.axis_index("y") * 4 + lax.axis_index("z") < Q
    factor = factor_ref[parity, u]
    lane = lax.broadcasted_iota(jnp.int32, (B, 128), 1)
    for c in range(COLS // CHUNK):
        product = jnp.dot(
            factor, gt_ref[:, c * CHUNK : (c + 1) * CHUNK], preferred_element_type=F32
        )
        for b in range(HALF):
            t = HALF * u + b
            keeps = mask_ref[pl.ds(2 * t + parity, 1), c * CHUNK : (c + 1) * CHUNK]
            for first, last in ((0, 128), (128, CHUNK)) if c == 0 else ((0, CHUNK),):
                cols = slice(c * CHUNK + first, c * CHUNK + last)
                part = product[b * B : b * B + B, first:last]
                keep = keeps[:, first:last]
                new = front_ref[t, parity, :, cols].astype(F32) - part * keep
                if cols.stop == 128:
                    new = jnp.where(owner & (lane < B), part, new)
                out_ref[b, 0, :, cols] = new.astype(BF16)


def update(front4, factor, columns, mask):
    whole = pl.BlockSpec(memory_space=VMEM)
    return pl.pallas_call(
        update_kernel,
        grid=(2, 2),
        out_shape=jax.ShapeDtypeStruct((PAIRS, 2, B, COLS), BF16),
        in_specs=[whole] * 4,
        out_specs=pl.BlockSpec((HALF, 1, B, COLS), lambda p, u: (u, p, 0, 0)),
        compiler_params=pltpu.CompilerParams(vmem_limit_bytes=20 << 20),
        cost_estimate=pl.CostEstimate(
            flops=2 * 3072 * 1536 * 256, bytes_accessed=4 * 3072 * 1536, transcendentals=0
        ),
    )(front4, factor, columns, mask)


def hand_on_kernel(in_ref, after_ref, out_ref):
    del after_ref
    out_ref[...] = in_ref[...]


def hand_on(message, after):
    whole = pl.BlockSpec(memory_space=VMEM)
    return pl.pallas_call(
        hand_on_kernel,
        out_shape=jax.ShapeDtypeStruct(message.shape, BF16),
        in_specs=[whole, pl.BlockSpec(memory_space=pl.ANY)],
        out_specs=whole,
        compiler_params=pltpu.CompilerParams(vmem_limit_bytes=8 << 20),
    )(message, after)


def body(front, diag_inverse, fill_pattern):
    front4 = front.reshape(PAIRS, 2, B, COLS)
    even, odd = pack(lax.slice(front, (0, 0), (front.shape[0], 128)).reshape(PAIRS, 2, B, 128))
    row_w, col_w, mask, stay = prepare(front4, diag_inverse, fill_pattern)
    spread = [
        lax.ppermute(part, ALL, spread_perm(k)) for k, part in enumerate((odd, even, odd))
    ]
    own = choose(even, *spread)
    mate = lax.ppermute(own, "z", [(0, 1), (1, 0), (2, 3), (3, 2)])
    pair = jnp.stack([own, mate])
    near = lax.ppermute(pair, ALL, column_perm())
    z_pair = lax.ppermute(pair, "z", [(1, 2), (2, 1), (3, 0), (0, 3)])
    y_next = lax.ppermute(pair, "y", [((i + 1) % 4, i) for i in range(4)])
    y_prev = lax.ppermute(pair, "y", [(i, (i + 1) % 4) for i in range(4)])
    far = lax.ppermute(hand_on(near, mask), "core", [(0, 1), (1, 0)])
    factor = row_factor((pair, z_pair, y_next, y_prev), row_w)
    columns = column_factor((near, far), col_w)
    out = update(stay, factor, columns, mask)
    return out.reshape(front.shape)


def solution(mesh):
    fine = Mesh(mesh.devices.reshape(4, 2, 4, 4), ALL)
    spec = P(("x", "core"), ("y", "z"))
    return jax.shard_map(
        body,
        mesh=fine,
        in_specs=(spec, P(), P()),
        out_specs=spec,
        check_vma=False,
    )
```

```python
import jax
import jax.numpy as jnp
from jax import lax
from jax.experimental import pallas as pl
from jax.experimental.pallas import tpu as pltpu
from jax.sharding import Mesh, PartitionSpec as P

BF16 = jnp.bfloat16
F32 = jnp.float32
B = 64
Q = 4
BLOCKS = 48
PAIRS = 24
HALF = 12
ROWS = HALF * B
COLS = 1536
WIDTH = 256
ALL = ("x", "core", "y", "z")
VMEM = pltpu.VMEM
NT = (((1,), (1,)), ((), ()))


def linear(x, core, y, z):
    return ((x * 2 + core) * 4 + y) * 4 + z


def quarter_of(y, z):
    return (z + 2 * (y // 2)) % 4


def spread_perm(step):
    pairs = []
    for x in range(4):
        for core in range(2):
            for j in range(4):
                target = [(1, j), (2, (j + 2) % 4), (3, (j + 2) % 4)][step]
                pairs.append((linear(x, core, 0, j), linear(x, core, *target)))
    return pairs


def column_perm():
    pairs = []
    for x in range(4):
        for core in range(2):
            r = 2 * x + core
            for y in range(4):
                for z in range(4):
                    to_x = (x - 2 * (y // 2) - z % 2) % 4
                    target = linear(to_x, quarter_of(y, z) // 2, 2 * (y % 2) + r // 4, r % 4)
                    pairs.append((linear(x, core, y, z), target))
    return pairs


def pack_kernel(panel_ref, even_ref, odd_ref):
    for parity, ref in enumerate((even_ref, odd_ref)):
        left = panel_ref[:HALF, parity, :, :].reshape(ROWS, 128)
        right = panel_ref[HALF:, parity, :, :].reshape(ROWS, 128)
        ref[...] = jnp.concatenate([left[:, :B], right[:, :B]], axis=1)


def pack(panel4):
    whole = pl.BlockSpec(memory_space=VMEM)
    return pl.pallas_call(
        pack_kernel,
        out_shape=(jax.ShapeDtypeStruct((ROWS, 128), BF16),) * 2,
        in_specs=[whole],
        out_specs=(whole,) * 2,
        compiler_params=pltpu.CompilerParams(vmem_limit_bytes=16 << 20),
    )(panel4)


def choose_kernel(a_ref, b_ref, c_ref, d_ref, own_ref):
    y = lax.axis_index("y")
    for k, ref in enumerate((a_ref, b_ref, c_ref, d_ref)):

        @pl.when(y == k)
        def _():
            own_ref[...] = ref[...]


def choose(a, b, c, d):
    whole = pl.BlockSpec(memory_space=VMEM)
    return pl.pallas_call(
        choose_kernel,
        out_shape=jax.ShapeDtypeStruct((ROWS, 128), BF16),
        in_specs=[whole] * 4,
        out_specs=whole,
        compiler_params=pltpu.CompilerParams(vmem_limit_bytes=16 << 20),
    )(a, b, c, d)


STAGES = 4


def prepare_kernel(
    front_ref, diag_ref, pattern_ref, row_w_ref, col_w_ref, mask_ref, stay_ref, sems
):
    span = PAIRS // STAGES
    copies = []
    for k in range(STAGES):
        part = pl.ds(k * span, span)
        copies.append(
            pltpu.make_async_copy(front_ref.at[part], stay_ref.at[part], sems.at[k])
        )
        copies[-1].start()
    x, core = lax.axis_index("x"), lax.axis_index("core")
    y, z = lax.axis_index("y"), lax.axis_index("z")
    own = lax.rem(z + 2 * (y // 2), 4)
    diag = diag_ref[...]
    eye = (
        lax.broadcasted_iota(jnp.int32, (WIDTH, WIDTH), 0)
        == lax.broadcasted_iota(jnp.int32, (WIDTH, WIDTH), 1)
    ).astype(BF16)
    turned = lax.dot_general(eye, diag, NT, preferred_element_type=F32).astype(BF16)
    bases = (own, lax.rem(own + 2 * lax.rem(y, 2), 4))
    source_x = 2 * lax.rem(y, 2) + z // 2
    swapped = lax.rem(x - source_x + 4, 2)
    for q in range(Q):
        part = turned[q * B : q * B + B, :]
        zero = jnp.zeros_like(part)
        for kind, base in enumerate(bases):
            slot = jnp.bitwise_xor(q, base)
            row_w_ref[kind, 0, slot] = jnp.concatenate([part, zero], axis=0)
            row_w_ref[kind, 1, slot] = jnp.concatenate([zero, part], axis=0)
        other = jnp.where(q // 2 == core, 0, 2)
        late = jnp.bitwise_xor(q % 2, swapped)
        part = diag[:, q * B : q * B + B]
        zero = jnp.zeros_like(part)
        col_w_ref[0, other + late] = jnp.concatenate([part, zero], axis=1)
        col_w_ref[1, other + late] = jnp.concatenate([zero, part], axis=1)
    row_id = x * 2 + core
    col_id = y * 4 + z
    count = pattern_ref.shape[0]
    rows = (
        lax.broadcasted_iota(jnp.int32, (BLOCKS, count), 0) * 8 + row_id
        == lax.broadcasted_iota(jnp.int32, (BLOCKS, count), 1)
    ).astype(BF16)
    cols = (
        lax.broadcasted_iota(jnp.int32, (count, COLS), 0)
        == lax.broadcasted_iota(jnp.int32, (count, COLS), 1) // B * 16 + col_id
    ).astype(BF16)
    picked = jnp.dot(
        rows, pattern_ref[...].astype(F32).astype(BF16), preferred_element_type=F32
    ).astype(BF16)
    keep = jnp.dot(picked, cols, preferred_element_type=F32)
    stored_row = lax.broadcasted_iota(jnp.int32, (BLOCKS, COLS), 0)
    stored_col = lax.broadcasted_iota(jnp.int32, (BLOCKS, COLS), 1) // B
    inside = (stored_row * 8 + row_id >= Q) & (stored_col * 16 + col_id >= Q)
    mask_ref[...] = jnp.where(inside, keep, 0.0)
    for copy in copies:
        copy.wait()


def prepare(front4, diag_inverse, fill_pattern):
    whole = pl.BlockSpec(memory_space=VMEM)
    return pl.pallas_call(
        prepare_kernel,
        out_shape=(
            jax.ShapeDtypeStruct((2, 2, Q, 128, WIDTH), BF16),
            jax.ShapeDtypeStruct((2, Q, WIDTH, 128), BF16),
            jax.ShapeDtypeStruct((BLOCKS, COLS), F32),
            jax.ShapeDtypeStruct(front4.shape, BF16),
        ),
        in_specs=[pl.BlockSpec(memory_space=pltpu.HBM), whole, whole],
        out_specs=(whole,) * 4,
        scratch_shapes=[pltpu.SemaphoreType.DMA((STAGES,))],
        compiler_params=pltpu.CompilerParams(vmem_limit_bytes=41 << 20),
        cost_estimate=pl.CostEstimate(
            flops=0, bytes_accessed=2 * 3072 * 1536 * 2, transcendentals=0
        ),
    )(front4, diag_inverse, fill_pattern)


def column_kernel(near_ref, far_ref, col_w_ref, out_ref):
    col_id = lax.axis_index("y") * 4 + lax.axis_index("z")
    for u in range(2):
        total = jnp.zeros((WIDTH, ROWS), F32)
        for k in range(Q):
            g = (near_ref, far_ref)[k // 2][k % 2]
            total += lax.dot_general(col_w_ref[u, k], g, NT, preferred_element_type=F32)
        out_ref[:, u * ROWS : (u + 1) * ROWS] = total.astype(BF16)

    @pl.when(col_id < Q)
    def _():
        lane = lax.broadcasted_iota(jnp.int32, (WIDTH, 128), 1)
        line = lax.broadcasted_iota(jnp.int32, (WIDTH, 128), 0)
        pick = (line == lane + col_id * B).astype(F32)
        old = out_ref[:, :128].astype(F32)
        out_ref[:, :128] = jnp.where(lane < B, pick, old).astype(BF16)


def column_factor(columns, col_w):
    whole = pl.BlockSpec(memory_space=VMEM)
    return pl.pallas_call(
        column_kernel,
        out_shape=jax.ShapeDtypeStruct((WIDTH, COLS), BF16),
        in_specs=[whole] * 3,
        out_specs=whole,
        compiler_params=pltpu.CompilerParams(vmem_limit_bytes=16 << 20),
        cost_estimate=pl.CostEstimate(
            flops=2 * COLS * 256 * 512, bytes_accessed=2 * COLS * 768, transcendentals=0
        ),
    )(*columns, col_w)


CHUNK = 512


def factor_kernel(own_ref, z_ref, next_ref, prev_ref, row_w_ref, out_ref):
    y = lax.axis_index("y")
    fours = (
        (own_ref[0], own_ref[1], z_ref[1], z_ref[0]),
        (next_ref[0], next_ref[1], prev_ref[0], prev_ref[1]),
    )
    for kind, four in enumerate(fours):
        parity = lax.rem(y + kind, 2)
        joined = jnp.concatenate(four, axis=1)
        for u in range(2):
            out_ref[parity, u] = jnp.dot(
                joined,
                row_w_ref[kind, u].reshape(Q * 128, WIDTH),
                preferred_element_type=F32,
            ).astype(BF16)


def row_factor(parts, row_w):
    whole = pl.BlockSpec(memory_space=VMEM)
    return pl.pallas_call(
        factor_kernel,
        out_shape=jax.ShapeDtypeStruct((2, 2, ROWS, WIDTH), BF16),
        in_specs=[whole] * 5,
        out_specs=whole,
        compiler_params=pltpu.CompilerParams(vmem_limit_bytes=16 << 20),
        cost_estimate=pl.CostEstimate(
            flops=2 * 3072 * 256 * 512, bytes_accessed=4 * 3072 * 256, transcendentals=0
        ),
    )(*parts, row_w)


def update_kernel(front_ref, factor_ref, gt_ref, mask_ref, out_ref):
    parity, u = pl.program_id(0), pl.program_id(1)
    owner = lax.axis_index("y") * 4 + lax.axis_index("z") < Q
    factor = factor_ref[parity, u]
    lane = lax.broadcasted_iota(jnp.int32, (B, 128), 1)
    for c in range(COLS // CHUNK):
        product = jnp.dot(
            factor, gt_ref[:, c * CHUNK : (c + 1) * CHUNK], preferred_element_type=F32
        )
        for b in range(HALF):
            t = HALF * u + b
            keeps = mask_ref[pl.ds(2 * t + parity, 1), c * CHUNK : (c + 1) * CHUNK]
            for first, last in ((0, 128), (128, CHUNK)) if c == 0 else ((0, CHUNK),):
                cols = slice(c * CHUNK + first, c * CHUNK + last)
                part = product[b * B : b * B + B, first:last]
                keep = keeps[:, first:last]
                new = front_ref[t, parity, :, cols].astype(F32) - part * keep
                if cols.stop == 128:
                    new = jnp.where(owner & (lane < B), part, new)
                out_ref[b, 0, :, cols] = new.astype(BF16)


def update(front4, factor, columns, mask):
    whole = pl.BlockSpec(memory_space=VMEM)
    return pl.pallas_call(
        update_kernel,
        grid=(2, 2),
        out_shape=jax.ShapeDtypeStruct((PAIRS, 2, B, COLS), BF16),
        in_specs=[whole] * 4,
        out_specs=pl.BlockSpec((HALF, 1, B, COLS), lambda p, u: (u, p, 0, 0)),
        compiler_params=pltpu.CompilerParams(vmem_limit_bytes=20 << 20),
        cost_estimate=pl.CostEstimate(
            flops=2 * 3072 * 1536 * 256, bytes_accessed=4 * 3072 * 1536, transcendentals=0
        ),
    )(front4, factor, columns, mask)


def hand_on_kernel(in_ref, after_ref, out_ref):
    del after_ref
    out_ref[...] = in_ref[...]


def hand_on(message, after):
    whole = pl.BlockSpec(memory_space=VMEM)
    return pl.pallas_call(
        hand_on_kernel,
        out_shape=jax.ShapeDtypeStruct(message.shape, BF16),
        in_specs=[whole, pl.BlockSpec(memory_space=pl.ANY)],
        out_specs=whole,
        compiler_params=pltpu.CompilerParams(vmem_limit_bytes=8 << 20),
    )(message, after)


def body(front, diag_inverse, fill_pattern):
    front4 = front.reshape(PAIRS, 2, B, COLS)
    even, odd = pack(lax.slice(front, (0, 0), (front.shape[0], 128)).reshape(PAIRS, 2, B, 128))
    row_w, col_w, mask, stay = prepare(front4, diag_inverse, fill_pattern)
    spread = [
        lax.ppermute(part, ALL, spread_perm(k)) for k, part in enumerate((odd, even, odd))
    ]
    own = choose(even, *spread)
    mate = lax.ppermute(own, "z", [(0, 1), (1, 0), (2, 3), (3, 2)])
    pair = jnp.stack([own, mate])
    near = lax.ppermute(pair, ALL, column_perm())
    z_pair = lax.ppermute(pair, "z", [(1, 2), (2, 1), (3, 0), (0, 3)])
    y_next = lax.ppermute(pair, "y", [((i + 1) % 4, i) for i in range(4)])
    y_prev = lax.ppermute(pair, "y", [(i, (i + 1) % 4) for i in range(4)])
    far = lax.ppermute(hand_on(near, mask), "core", [(0, 1), (1, 0)])
    factor = row_factor((pair, z_pair, y_next, y_prev), row_w)
    columns = column_factor((near, far), col_w)
    out = update(stay, factor, columns, mask)
    return out.reshape(front.shape)


def solution(mesh):
    fine = Mesh(mesh.devices.reshape(4, 2, 4, 4), ALL)
    spec = P(("x", "core"), ("y", "z"))
    return jax.shard_map(
        body,
        mesh=fine,
        in_specs=(spec, P(), P()),
        out_specs=spec,
        check_vma=False,
    )
```
